128 devices in a mesh: blk: 16 (over z, y), cuts: 8 (over x, core).
Axes of the slice: x: 4, y: 4, z: 4, core: 2. Of those that a mesh axis runs over, the one named last changes fastest.
Arguments:
- integrals: bfloat16 [128, 4096, 3072], P('blk', None, 'cuts'), may hold values from -0.0234375 to 0.0234375
- amplitudes: bfloat16 [128, 128, 4096], P('blk', 'cuts'), may hold values from -6 to 6
- tile_index: int32 [128], replicated, may hold values from 0 to 127, as said below
- live_blocks: int32 [16], replicated, may hold values from 1 to 8, as said below
- pair_index: int32 [128, 2], replicated, may hold values from 0 to 159
- occ_energy: float32 [160], replicated, may hold values from -2 to -0.5
- ab_energy: float32 [3072], P('cuts'), may hold values from 0.5 to 4
Outputs:
- update: float32 [128, 3072], P(None, 'cuts')
The draws below stay inside these ranges and needn't reach their ends.
Inputs may be any that keep to these rules, and one draw needn't show every extreme that they name: `tile_index`: A permutation of the stored tiles. Of the 8 slots of one group, at most 2 pair with tiles stored in one group (tile t is stored in group t // 8), and some group and store pair exactly 2 times. `live_blocks`: some group has all 8 slots live.
All inputs are finite; a program needn't handle non-finite values.
Results may differ from the reference program's by a relative error of at most 0.0003.
Values may be sent and summed in bfloat16 or wider, within the bound.
A program may use at most 192 MiB of HBM per device.

```python
import jax
import jax.numpy as jnp
from jax import lax

TILE2 = 4096
NOCC = 160
PAIRS = 128
BLK_DEV = 8
GROUPS = 16
NBLK = 128
AB = 3072


def draw_tile_index(key, part):
    key = jax.random.fold_in(key, 11)
    subkeys = jax.random.split(key, 6)
    groups = NBLK // BLK_DEV
    doubled = jax.random.randint(subkeys[0], (), 0, groups)
    others = (doubled + 1 + jnp.arange(2 * (groups - 1)) % (groups - 1)) % groups
    others = jax.random.permutation(subkeys[1], others)
    offsets = jnp.concatenate([jnp.stack([doubled, doubled]), others[:BLK_DEV - 2]])
    offsets = jax.random.permutation(subkeys[2], offsets)
    receiver_order = jax.random.permutation(subkeys[3], groups)
    owner_order = jax.random.permutation(subkeys[4], groups)
    slot_orders = jax.vmap(lambda single: jax.random.permutation(single, BLK_DEV))(jax.random.split(subkeys[5], groups))
    owner_group = owner_order[(receiver_order[:, None] + offsets[None, :]) % groups]
    owner_slot = slot_orders[owner_group, jnp.arange(BLK_DEV)[None, :]]
    return (owner_group * BLK_DEV + owner_slot).reshape(-1).astype(jnp.int32)


def draw_live_blocks(key, part):
    key = jax.random.fold_in(key, 12)
    subkeys = jax.random.split(key, 2)
    lowest = max(1, 3 * BLK_DEV // 4)
    live_counts = jax.random.randint(subkeys[0], (GROUPS,), lowest, BLK_DEV + 1)
    busiest = jax.random.randint(subkeys[1], (), 0, GROUPS)
    return jnp.where(jnp.arange(GROUPS) == busiest, BLK_DEV, live_counts).astype(jnp.int32)


def with_ends(array, stream_key, least, high):
    spot = [jax.random.randint(jax.random.fold_in(stream_key, axis), (), 0, length) for axis, length in enumerate(array.shape)]
    longest = array.shape.index(max(array.shape))
    neighbour = spot[:longest] + [(spot[longest] + 1) % array.shape[longest]] + spot[longest + 1:]
    return array.at[tuple(spot)].set(least).at[tuple(neighbour)].set(high)


def spiked(entries, key, source, target, parts, factor):
    def block_of(position):
        return (jnp.arange(entries.shape[position]) // (entries.shape[position] // parts)).reshape((-1,) + (1,) * (entries.ndim - 1 - position))

    one_side = jax.random.permutation(key, parts)[block_of(target)]
    far = (block_of(target) + parts // 2) % parts
    return jnp.where((block_of(source) == one_side) | (block_of(source) == far), factor * entries, entries)


def levels(own_key, shape, shards, smallest, largest):
    level = 1.0
    for position, blocks in shards:
        draws = jax.random.uniform(jax.random.fold_in(jax.random.fold_in(own_key, 6), position), (blocks,), jnp.float32, smallest / len(shards), largest / len(shards))
        level = level * jnp.repeat(jnp.exp(draws), shape[position] // blocks).reshape((-1,) + (1,) * (len(shape) - 1 - position))
    return level


def scatter_about(stream_key, dims, width, limit, cuts=(), kind=jnp.bfloat16):
    entries = width * jax.random.normal(stream_key, dims, jnp.float32)
    if cuts:
        entries = entries * levels(stream_key, dims, cuts, -0.22, 0.18)
    return jnp.clip(entries, -limit, limit).astype(kind)


def noise_with(own_key, shape, scale, bound, shards, heavy, kind=jnp.bfloat16):
    drawn = scale * jax.random.normal(own_key, shape, jnp.float32)
    if shards:
        drawn = drawn * levels(own_key, shape, shards, -0.22, 0.18)
    return jnp.clip(spiked(drawn, jax.random.fold_in(own_key, 3), *heavy), -bound, bound).astype(kind)


def setup_inputs(seed: int = 0) -> dict:
    keys = jax.random.split(jax.random.key(seed), 8)
    integrals = scatter_about(keys[0], (NBLK, TILE2, AB), (TILE2 * NBLK // 8) ** -0.5, 0.0234375, ((0, 16), (2, 8)))
    amplitudes = noise_with(keys[1], (NBLK, PAIRS, TILE2), 1.0, 6.0, ((0, 16), (1, 8)), (0, 1, 16, 2.0))
    tile_index = draw_tile_index(jax.random.fold_in(keys[7], 71), 0)
    live_blocks = draw_live_blocks(jax.random.fold_in(keys[7], 71), 0)
    pair_index = with_ends(jax.random.randint(keys[4], (PAIRS, 2), 0, NOCC), jax.random.fold_in(keys[4], 1), 0, NOCC - 1).astype(jnp.int32)
    occ_energy = jnp.clip(jax.random.uniform(keys[5], (NOCC,), jnp.float32, -2.0, -0.5), -2.0, -0.5)
    ab_energy = jnp.clip(0.5 + 3.5 * jax.random.uniform(keys[6], (AB,), jnp.float32) ** levels(keys[6], (AB,), ((0, 8),), -0.2, 0.2), 0.5, 4.0)
    return {"integrals": integrals, "amplitudes": amplitudes, "tile_index": tile_index, "live_blocks": live_blocks, "pair_index": pair_index, "occ_energy": occ_energy, "ab_energy": ab_energy}


def reference(integrals, amplitudes, tile_index, live_blocks, pair_index, occ_energy, ab_energy):
    def visit(running, block_slot):
        is_live = (block_slot % BLK_DEV) < live_blocks[block_slot // BLK_DEV]

        def add_block(partial_sum):
            tile_rows = amplitudes[tile_index[block_slot]]
            return partial_sum + jnp.dot(tile_rows, integrals[block_slot], preferred_element_type=jnp.float32)

        def keep_sum(partial_sum):
            return partial_sum

        return lax.cond(is_live, add_block, keep_sum, running), None

    ladder, _ = lax.scan(visit, jnp.zeros((PAIRS, AB), jnp.float32), jnp.arange(NBLK, dtype=jnp.int32))
    first_energy = occ_energy[pair_index[:, 0]]
    second_energy = occ_energy[pair_index[:, 1]]
    denominator = first_energy[:, None] + second_energy[:, None] - ab_energy[None, :]
    return ladder / denominator
```

```python
import jax
import jax.numpy as jnp
from jax import lax
from jax.sharding import PartitionSpec as P

MOST = 2


def on_device(integrals, amplitudes, tile_index, live_blocks, pair_index, occ_energy, ab_energy):
    groups = lax.axis_size("blk")
    own_group = lax.axis_index("blk")
    per_group = integrals.shape[0]
    owner_grid = (tile_index // per_group).reshape(groups, per_group)
    slot_grid = (tile_index % per_group).reshape(groups, per_group)
    positions = jnp.arange(per_group, dtype=jnp.int32)
    same_owner = owner_grid[:, :, None] == owner_grid[:, None, :]
    earlier = positions[None, :] < positions[:, None]
    rank_grid = jnp.sum((same_owner & earlier[None, :, :]).astype(jnp.int32), axis=2)
    chosen = owner_grid == own_group
    slot_numbers = jnp.arange(MOST, dtype=jnp.int32)
    picked = chosen[:, None, :] & (rank_grid[:, None, :] == slot_numbers[None, :, None])
    send_tile = jnp.sum(jnp.where(picked, slot_grid[:, None, :], 0), axis=2).reshape(-1)
    my_owner = lax.dynamic_index_in_dim(owner_grid, own_group, 0, keepdims=False)
    my_rank = lax.dynamic_index_in_dim(rank_grid, own_group, 0, keepdims=False)
    receive_row = my_owner * MOST + my_rank
    selected = jnp.take(amplitudes, send_tile, axis=0)
    received = lax.all_to_all(selected, "blk", split_axis=0, concat_axis=0, tiled=True)
    own_rows = jnp.take(received, receive_row, axis=0)
    needed = lax.all_gather(own_rows, "cuts", axis=1, tiled=True)
    live_count = lax.dynamic_index_in_dim(live_blocks, own_group, 0, keepdims=False)

    def accumulate(block_slot, running):
        tile_rows = lax.dynamic_index_in_dim(needed, block_slot, 0, keepdims=False)
        block_cols = lax.dynamic_index_in_dim(integrals, block_slot, 0, keepdims=False)
        return running + jnp.dot(tile_rows, block_cols, preferred_element_type=jnp.float32)

    partial_sum = lax.fori_loop(
        0, live_count, accumulate, jnp.zeros((needed.shape[1], integrals.shape[2]), jnp.float32)
    )
    orbitals = jnp.arange(occ_energy.shape[0], dtype=jnp.int32)
    first_energy = jnp.sum(
        jnp.where(pair_index[:, 0:1] == orbitals[None, :], occ_energy[None, :], 0.0), axis=1
    )
    second_energy = jnp.sum(
        jnp.where(pair_index[:, 1:2] == orbitals[None, :], occ_energy[None, :], 0.0), axis=1
    )
    denominator = first_energy[:, None] + second_energy[:, None] - ab_energy[None, :]
    ladder = lax.psum(partial_sum, "blk")
    return ladder / denominator


def solution(mesh):
    in_specs = (P("blk", None, "cuts"), P("blk", "cuts", None), P(), P(), P(), P(), P("cuts"))
    out_specs = P(None, "cuts")
    return jax.shard_map(
        on_device, mesh=mesh, in_specs=in_specs, out_specs=out_specs, check_vma=False
    )
```

```python
import functools

import jax
import jax.numpy as jnp
from jax import lax
from jax.experimental import pallas as pl
from jax.experimental.pallas import tpu as pltpu
from jax.sharding import PartitionSpec as P

MOST = 2
WIDTHS = (512,) * 8
AHEAD = 2
MESH = pl.DeviceIdType.MESH


def moved(group, offset, sign):
    z = (group // 4 + sign * (offset // 4) + 4) % 4
    y = (group % 4 + sign * (offset % 4) + 4) % 4
    return z * 4 + y


def kernel(widths, *refs):
    parts = len(widths)
    starts = [sum(widths[:j]) for j in range(parts)]
    (send_pick, take_pick, live, pairs, occ, ab, integrals, amplitudes, out, tiles, total, sums, summed) = refs[:13]
    rest = refs[13:]
    blocks, leave, land, rows = (rest[i * parts:(i + 1) * parts] for i in range(4))
    (tile_sem, block_sem, leave_sem, land_sem, way_sem, from_low, from_high, from_low2, from_high2, from_twin,
     sum_send, sum_recv, out_send, out_recv, end_sem) = rest[4 * parts:]
    groups, cuts = lax.axis_size("blk"), lax.axis_size("cuts")
    group, cut = lax.axis_index("blk"), lax.axis_index("cuts")
    high, low, twin = (cut + 2) % cuts, (cut + cuts - 2) % cuts, cut + 1 - 2 * (cut % 2)
    far = (cut + 4) % cuts

    tile_copy = pltpu.make_async_copy(amplitudes, tiles, tile_sem)
    tile_copy.start()

    def block_copy(j):
        return pltpu.make_async_copy(integrals.at[:, pl.ds(starts[j], widths[j]), :], blocks[j], block_sem.at[j])

    for j in range(parts):
        block_copy(j).start()

    barrier = pltpu.get_barrier_semaphore()

    def greet(offset, carry):
        pl.semaphore_signal(barrier, inc=1, device_id={"blk": moved(group, offset, 1), "cuts": cut}, device_id_type=MESH)
        return carry

    lax.fori_loop(1, groups, greet, 0)
    for other in (high, low, twin):
        pl.semaphore_signal(barrier, inc=1, device_id={"blk": group, "cuts": other}, device_id_type=MESH)
    pl.semaphore_wait(barrier, groups - 1 + 3)
    tile_copy.wait()

    def spread(j):
        columns = pl.ds(starts[j], widths[j])
        for rank in range(MOST):
            land[j][rank] = tiles[send_pick[rank], :, columns]

        def one(offset, carry):
            for rank in range(MOST):
                leave[j][offset * MOST + rank] = tiles[send_pick[offset * MOST + rank], :, columns]
            place = pl.ds(offset * MOST, MOST)
            pltpu.make_async_remote_copy(
                src_ref=leave[j].at[place],
                dst_ref=land[j].at[place],
                send_sem=leave_sem.at[j],
                recv_sem=land_sem.at[j],
                device_id={"blk": moved(group, offset, 1), "cuts": cut},
                device_id_type=MESH,
            ).start()
            return carry

        lax.fori_loop(1, groups, one, 0)

    def along(j, owner, target, arrival, half=None):
        width = 8 * widths[j]
        columns = pl.ds(0, width) if half is None else pl.ds(half * (width // 2), width // 2)
        view = rows[j].at[pl.ds(pl.multiple_of(owner * 16, 16), 16), columns]
        return pltpu.make_async_remote_copy(
            src_ref=view,
            dst_ref=view,
            send_sem=way_sem.at[j],
            recv_sem=arrival.at[j],
            device_id={"blk": group, "cuts": target},
            device_id_type=MESH,
        )

    def wait_for(ref, semaphore):
        pltpu.make_async_copy(ref, ref, semaphore).wait()

    def piece(j, half=False):
        return rows[j].at[pl.ds(0, 16), pl.ds(0, 8 * widths[j] // (2 if half else 1))]

    def turn(j):
        wait_for(land[j].at[pl.ds(MOST, (groups - 1) * MOST)], land_sem.at[j])
        mine = pl.ds(pl.multiple_of(cut * 16, 16), 16)
        for block in range(8):
            tile = land[j][take_pick[block]]
            kept = jnp.where(live[block] > 0, tile, jnp.zeros_like(tile))
            rows[j][mine, pl.ds(block * widths[j], widths[j])] = kept
        along(j, cut, high, from_low).start()
        along(j, cut, low, from_high).start()
        along(j, cut, twin, from_twin).start()

    def relay(j):
        wait_for(piece(j), from_low.at[j])
        along(j, low, high, from_low2, 0).start()
        along(j, low, twin, from_twin).start()
        wait_for(piece(j), from_high.at[j])
        along(j, high, low, from_high2, 1).start()
        along(j, high, twin, from_twin).start()

    def finish(j):
        wait_for(piece(j, True), from_low2.at[j])
        along(j, far, twin, from_twin, 0).start()
        wait_for(piece(j, True), from_high2.at[j])
        along(j, far, twin, from_twin, 1).start()

    def multiply(j):
        wait_for(rows[j].at[pl.ds(0, 64)], from_twin.at[j])
        block_copy(j).wait()
        block = blocks[j][...].reshape(8 * widths[j], blocks[j].shape[2])
        product = jnp.dot(rows[j][...], block, preferred_element_type=jnp.float32)
        product = product.reshape(total.shape)
        if j == 0:
            total[...] = product
        else:
            total[...] += product

    for j in range(min(AHEAD, parts)):
        spread(j)
    for t in range(parts + 3):
        if t + AHEAD < parts:
            spread(t + AHEAD)
        if t < parts:
            turn(t)
        if 0 <= t - 1 < parts:
            relay(t - 1)
        if 0 <= t - 2 < parts:
            finish(t - 2)
        if 0 <= t - 3 < parts:
            multiply(t - 3)

    def scatter(offset, carry):
        target = moved(group, offset, 1)
        pltpu.make_async_remote_copy(
            src_ref=total.at[target],
            dst_ref=sums.at[offset],
            send_sem=sum_send,
            recv_sem=sum_recv,
            device_id={"blk": target, "cuts": cut},
            device_id_type=MESH,
        ).start()
        return carry

    lax.fori_loop(1, groups, scatter, 0)
    own_pairs = pairs[pl.ds(pl.multiple_of(group * 8, 8), 8), :]
    orbitals = lax.broadcasted_iota(jnp.int32, (8, occ.shape[1]), 1)
    energies = jnp.broadcast_to(occ[...], orbitals.shape)
    first = jnp.sum(jnp.where(own_pairs[:, 0:1] == orbitals, energies, 0.0), axis=1, keepdims=True)
    second = jnp.sum(jnp.where(own_pairs[:, 1:2] == orbitals, energies, 0.0), axis=1, keepdims=True)
    denominator = first + second - ab[...]
    wait_for(sums.at[pl.ds(1, groups - 1)], sum_recv)
    ladder = total[group]
    for offset in range(1, groups):
        ladder = ladder + sums[offset]
    summed[group] = ladder / denominator

    def share(offset, carry):
        pltpu.make_async_remote_copy(
            src_ref=summed.at[group],
            dst_ref=summed.at[group],
            send_sem=out_send,
            recv_sem=out_recv,
            device_id={"blk": moved(group, offset, 1), "cuts": cut},
            device_id_type=MESH,
        ).start()
        return carry

    lax.fori_loop(1, groups, share, 0)
    for j in range(parts):
        wait_for(leave[j].at[pl.ds(MOST, (groups - 1) * MOST)], leave_sem.at[j])
        wait_for(rows[j].at[pl.ds(0, 112)], way_sem.at[j])
    wait_for(sums.at[pl.ds(1, groups - 1)], sum_send)
    wait_for(sums.at[pl.ds(1, groups - 1)], out_recv)
    end = pltpu.make_async_copy(summed, out, end_sem)
    end.start()
    wait_for(sums.at[pl.ds(1, groups - 1)], out_send)
    end.wait()


def on_device(integrals, amplitudes, tile_index, live_blocks, pair_index, occ_energy, ab_energy):
    groups = lax.axis_size("blk")
    group = lax.axis_index("blk")
    per_group, depth, width = integrals.shape
    owner = tile_index // per_group
    slot = tile_index % per_group
    grid = owner.reshape(groups, per_group)
    positions = jnp.arange(per_group, dtype=jnp.int32)
    earlier = positions[None, :] < positions[:, None]
    rank = jnp.sum(((grid[:, :, None] == grid[:, None, :]) & earlier[None]).astype(jnp.int32), axis=2).reshape(-1)
    holder = jnp.arange(groups * per_group, dtype=jnp.int32) // per_group
    onward = moved(holder, group, -1)
    entry = onward * MOST + rank
    entries = jnp.arange(groups * MOST, dtype=jnp.int32)
    send_pick = jnp.sum(jnp.where((owner == group)[None] & (entry[None] == entries[:, None]), slot[None], 0), axis=1)
    backward = moved(group, owner, -1)
    take_pick = lax.dynamic_slice_in_dim(backward * MOST + rank, group * per_group, per_group)
    live = (positions < lax.dynamic_index_in_dim(live_blocks, group, 0, keepdims=False)).astype(jnp.int32)

    rows, parts = amplitudes.shape[1], len(WIDTHS)
    pairs = rows * lax.axis_size("cuts")
    part_rows = pairs // groups
    smem, vmem, hbm = (pl.BlockSpec(memory_space=space) for space in (pltpu.SMEM, pltpu.VMEM, pl.ANY))
    dma = pltpu.SemaphoreType.DMA
    scratch = [
        pltpu.VMEM(amplitudes.shape, jnp.bfloat16),
        pltpu.VMEM((groups, part_rows, width), jnp.float32),
        pltpu.VMEM((groups, part_rows, width), jnp.float32),
        pltpu.VMEM((groups, part_rows, width), jnp.float32),
    ]
    scratch += [pltpu.VMEM((per_group, each, width), jnp.bfloat16) for each in WIDTHS]
    scratch += [pltpu.VMEM((groups * MOST, rows, each), jnp.bfloat16) for each in WIDTHS] * 2
    scratch += [pltpu.VMEM((pairs, per_group * each), jnp.bfloat16) for each in WIDTHS]
    scratch += [dma] + [dma((parts,))] * 9 + [dma] * 5
    update = pl.pallas_call(
        functools.partial(kernel, WIDTHS),
        out_shape=jax.ShapeDtypeStruct((groups, part_rows, width), jnp.float32),
        in_specs=[smem, smem, smem, vmem, vmem, vmem, hbm, hbm],
        out_specs=hbm,
        scratch_shapes=scratch,
        compiler_params=pltpu.CompilerParams(collective_id=0, has_side_effects=True, vmem_limit_bytes=56 << 20),
        cost_estimate=pl.CostEstimate(flops=2 * pairs * per_group * depth * width, bytes_accessed=integrals.size * 2, transcendentals=0),
        name="ladder",
    )(send_pick, take_pick, live, pair_index, occ_energy[None], ab_energy[None], integrals, amplitudes)
    return update.reshape(pairs, width)


def solution(mesh):
    in_specs = (P("blk", None, "cuts"), P("blk", "cuts", None), P(), P(), P(), P(), P("cuts"))
    out_specs = P(None, "cuts")
    return jax.shard_map(
        on_device, mesh=mesh, in_specs=in_specs, out_specs=out_specs, check_vma=False
    )
```

```python
import functools

import jax
import jax.numpy as jnp
from jax import lax
from jax.experimental import pallas as pl
from jax.experimental.pallas import tpu as pltpu
from jax.sharding import PartitionSpec as P

LANES = 128
PIECES = 4
SPREAD_AHEAD = 4
SORT_AHEAD = 2
MESH = pl.DeviceIdType.MESH


def moved(group, offset):
    z = (group // 4 + offset // 4) % 4
    y = (group % 4 + offset % 4) % 4
    return z * 4 + y


def kernel(parts, *refs):
    (tile_index, live_blocks, pairs, occ, ab, integrals, amplitudes, out) = refs[:8]
    (tiles, total, sums, summed) = refs[8:12]
    middle, leave = refs[12:14], refs[14:16]
    blocks, rows = refs[16:16 + parts], refs[16 + parts:16 + 2 * parts]
    (tile_sem, block_sem, spread_send, spread_recv, sort_send, sort_recv, way_sem, from_low, from_high, from_low2,
     from_high2, from_twin, sum_send, sum_recv, out_send, out_recv, end_sem) = refs[16 + 2 * parts:]
    groups, cuts = lax.axis_size("blk"), lax.axis_size("cuts")
    group, cut = lax.axis_index("blk"), lax.axis_index("cuts")
    high, low, twin = (cut + 2) % cuts, (cut + cuts - 2) % cuts, cut + 1 - 2 * (cut % 2)
    far = (cut + 4) % cuts
    width = integrals.shape[2]
    span = 8 * LANES

    tile_copy = pltpu.make_async_copy(amplitudes, tiles, tile_sem)
    tile_copy.start()

    barrier = pltpu.get_barrier_semaphore()

    def greet(offset, carry):
        pl.semaphore_signal(barrier, inc=1, device_id={"blk": moved(group, offset), "cuts": cut}, device_id_type=MESH)
        return carry

    lax.fori_loop(1, groups, greet, 0)
    for other in (high, low, twin):
        pl.semaphore_signal(barrier, inc=1, device_id={"blk": group, "cuts": other}, device_id_type=MESH)
    pl.semaphore_wait(barrier, groups - 1 + 3)
    tile_copy.wait()

    def wait_for(ref, semaphore):
        pltpu.make_async_copy(ref, ref, semaphore).wait()

    def block_copy(j, k):
        return pltpu.make_async_copy(
            integrals.at[:, pl.ds((j * PIECES + k) * LANES, LANES), :], blocks[j].at[pl.ds(k * 8, 8)], block_sem.at[j]
        )

    def spread(j):
        half = j // 4
        for k in range(PIECES):
            hub = k * 4 + (k + j) % 4
            source = tiles.at[:, :, pl.ds((j * PIECES + k) * LANES, LANES)]
            place = middle[half].at[pl.ds(pl.multiple_of(group * 8, 8), 8)]

            @pl.when(group == hub)
            def _():
                pltpu.make_async_copy(source, place, spread_recv.at[half]).start()

            @pl.when(group != hub)
            def _():
                pltpu.make_async_remote_copy(
                    src_ref=source,
                    dst_ref=place,
                    send_sem=spread_send.at[half],
                    recv_sem=spread_recv.at[half],
                    device_id={"blk": hub, "cuts": cut},
                    device_id_type=MESH,
                ).start()

    def sort(j):
        half = j // 4

        @pl.when(group % 4 == (group // 4 + j) % 4)
        def _():
            wait_for(middle[half], spread_recv.at[half])
            place = rows[j].at[pl.ds(pl.multiple_of(cut * 16, 16), 16), pl.ds(pl.multiple_of(group // 4 * span, span), span)]

            def pick(offset):
                target = moved(group, offset)
                live = live_blocks[target]
                for block in range(8):
                    tile = middle[half][tile_index[target * 8 + block]]
                    kept = jnp.where(live > block, tile, jnp.zeros_like(tile))
                    leave[half][offset, :, pl.ds(block * LANES, LANES)] = kept
                return target

            def one(offset, carry):
                target = pick(offset)
                pltpu.make_async_remote_copy(
                    src_ref=leave[half].at[offset],
                    dst_ref=place,
                    send_sem=sort_send.at[half],
                    recv_sem=sort_recv.at[j],
                    device_id={"blk": target, "cuts": cut},
                    device_id_type=MESH,
                ).start()
                return carry

            lax.fori_loop(1, groups, one, 0)
            pick(0)
            pltpu.make_async_copy(leave[half].at[0], place, sort_recv.at[j]).start()

    def along(j, owner, target, arrival, half=None):
        columns = pl.ds(0, PIECES * span) if half is None else pl.ds(half * (PIECES * span // 2), PIECES * span // 2)
        view = rows[j].at[pl.ds(pl.multiple_of(owner * 16, 16), 16), columns]
        return pltpu.make_async_remote_copy(
            src_ref=view,
            dst_ref=view,
            send_sem=way_sem.at[j],
            recv_sem=arrival.at[j],
            device_id={"blk": group, "cuts": target},
            device_id_type=MESH,
        )

    def piece(j, half=False):
        return rows[j].at[pl.ds(0, 16), pl.ds(0, PIECES * span // (2 if half else 1))]

    def turn(j):
        wait_for(piece(j), sort_recv.at[j])
        along(j, cut, high, from_low).start()
        along(j, cut, low, from_high).start()
        along(j, cut, twin, from_twin).start()
        for k in range(PIECES):
            block_copy(j, k).start()

    def relay(j):
        wait_for(piece(j), from_low.at[j])
        along(j, low, high, from_low2, 0).start()
        along(j, low, twin, from_twin).start()
        wait_for(piece(j), from_high.at[j])
        along(j, high, low, from_high2, 1).start()
        along(j, high, twin, from_twin).start()

    def finish(j):
        wait_for(piece(j, True), from_low2.at[j])
        along(j, far, twin, from_twin, 0).start()
        wait_for(piece(j, True), from_high2.at[j])
        along(j, far, twin, from_twin, 1).start()

    def multiply(j):
        wait_for(rows[j].at[pl.ds(0, 64)], from_twin.at[j])
        wait_for(blocks[j], block_sem.at[j])
        block = blocks[j][...].reshape(PIECES * span, width)
        product = jnp.dot(rows[j][...], block, preferred_element_type=jnp.float32)
        product = product.reshape(total.shape)
        if j == 0:
            total[...] = product
        else:
            total[...] += product

    for j in range(min(SPREAD_AHEAD, parts)):
        spread(j)
    for j in range(min(SORT_AHEAD, parts)):
        sort(j)
    for t in range(parts + 3):
        if t + SPREAD_AHEAD < parts:
            spread(t + SPREAD_AHEAD)
        if t + SORT_AHEAD < parts:
            sort(t + SORT_AHEAD)
        if t < parts:
            turn(t)
        if 0 <= t - 1 < parts:
            relay(t - 1)
        if 0 <= t - 2 < parts:
            finish(t - 2)
        if 0 <= t - 3 < parts:
            multiply(t - 3)

    def scatter(offset, carry):
        target = moved(group, offset)
        pltpu.make_async_remote_copy(
            src_ref=total.at[target],
            dst_ref=sums.at[offset],
            send_sem=sum_send,
            recv_sem=sum_recv,
            device_id={"blk": target, "cuts": cut},
            device_id_type=MESH,
        ).start()
        return carry

    lax.fori_loop(1, groups, scatter, 0)
    line = lax.broadcasted_iota(jnp.int32, (8, width), 0)
    energy = jnp.zeros((8, width), jnp.float32)
    for i in range(8):
        pair = group * 8 + i
        energy = jnp.where(line == i, occ[pairs[0, pair]] + occ[pairs[1, pair]], energy)
    denominator = energy - ab[...].reshape(1, width)
    wait_for(sums.at[pl.ds(1, groups - 1)], sum_recv)
    ladder = total[group]
    for offset in range(1, groups):
        ladder = ladder + sums[offset]
    summed[group] = ladder / denominator

    def share(offset, carry):
        pltpu.make_async_remote_copy(
            src_ref=summed.at[group],
            dst_ref=summed.at[group],
            send_sem=out_send,
            recv_sem=out_recv,
            device_id={"blk": moved(group, offset), "cuts": cut},
            device_id_type=MESH,
        ).start()
        return carry

    lax.fori_loop(1, groups, share, 0)
    for half in range(2):
        wait_for(middle[half].at[pl.ds(8, 120)], spread_send.at[half])
        wait_for(leave[half].at[pl.ds(1, groups - 1)], sort_send.at[half])
    for j in range(parts):
        wait_for(rows[j].at[pl.ds(0, 112)], way_sem.at[j])
    wait_for(sums.at[pl.ds(1, groups - 1)], sum_send)
    wait_for(sums.at[pl.ds(1, groups - 1)], out_recv)
    end = pltpu.make_async_copy(summed, out, end_sem)
    end.start()
    wait_for(sums.at[pl.ds(1, groups - 1)], out_send)
    end.wait()


def on_device(integrals, amplitudes, tile_index, live_blocks, pair_index, occ_energy, ab_energy):
    groups = lax.axis_size("blk")
    per_group, depth, width = integrals.shape
    rows = amplitudes.shape[1]
    pairs = rows * lax.axis_size("cuts")
    part_rows = pairs // groups
    parts = depth // (LANES * PIECES)
    smem, vmem, hbm = (pl.BlockSpec(memory_space=space) for space in (pltpu.SMEM, pltpu.VMEM, pl.ANY))
    dma = pltpu.SemaphoreType.DMA
    scratch = [pltpu.VMEM(amplitudes.shape, jnp.bfloat16)]
    scratch += [pltpu.VMEM((groups, part_rows, width), jnp.float32)] * 3
    scratch += [pltpu.VMEM((groups * per_group, rows, LANES), jnp.bfloat16)] * 2
    scratch += [pltpu.VMEM((groups, rows, per_group * LANES), jnp.bfloat16)] * 2
    scratch += [pltpu.VMEM((PIECES * per_group, LANES, width), jnp.bfloat16)] * parts
    scratch += [pltpu.VMEM((pairs, PIECES * per_group * LANES), jnp.bfloat16)] * parts
    scratch += [dma, dma((parts,)), dma((2,)), dma((2,)), dma((2,)), dma((parts,))] + [dma((parts,))] * 6 + [dma] * 5
    update = pl.pallas_call(
        functools.partial(kernel, parts),
        out_shape=jax.ShapeDtypeStruct((groups, part_rows, width), jnp.float32),
        in_specs=[smem, smem, smem, smem, vmem, hbm, hbm],
        out_specs=hbm,
        scratch_shapes=scratch,
        compiler_params=pltpu.CompilerParams(collective_id=0, has_side_effects=True, vmem_limit_bytes=56 << 20),
        cost_estimate=pl.CostEstimate(flops=2 * pairs * per_group * depth * width, bytes_accessed=integrals.size * 2, transcendentals=0),
        name="ladder",
    )(tile_index, live_blocks, pair_index.T, occ_energy, ab_energy, integrals, amplitudes)
    return update.reshape(pairs, width)


def solution(mesh):
    in_specs = (P("blk", None, "cuts"), P("blk", "cuts", None), P(), P(), P(), P(), P("cuts"))
    out_specs = P(None, "cuts")
    return jax.shard_map(
        on_device, mesh=mesh, in_specs=in_specs, out_specs=out_specs, check_vma=False
    )
```

```python
import functools

import jax
import jax.numpy as jnp
from jax import lax
from jax.experimental import pallas as pl
from jax.experimental.pallas import tpu as pltpu
from jax.sharding import PartitionSpec as P

LANES = 128
QUARTERS = 4
HUBS = 8
CHUNKS = tuple((quarter, first, 4) for quarter in range(QUARTERS) for first in range(0, 8, 4))
SORT_AHEAD = 2
STRIDE = 5
MESH = pl.DeviceIdType.MESH


def moved(group, offset):
    return ((group + (offset & 12)) & 12) | ((group + offset) & 3)


def kernel(chunks, *refs):
    parts = len(chunks)
    (tile_index, live_blocks, pairs, occ, ab, integrals, amplitudes, out) = refs[:8]
    (tiles, total, sums, mine) = refs[8:12]
    middle, leave = refs[12:14], refs[14:16]
    blocks, rows = refs[16:16 + parts], refs[16 + parts:16 + 2 * parts]
    (tile_sem, block_sem, spread_send, spread_recv, sort_send, sort_recv, way_sem, from_low, from_high, from_low2,
     from_high2, from_twin, sum_send, sum_recv, out_send, out_recv, end_sem) = refs[16 + 2 * parts:]
    groups, cuts = lax.axis_size("blk"), lax.axis_size("cuts")
    group, cut = lax.axis_index("blk"), lax.axis_index("cuts")
    high, low, twin = (cut + 2) & (cuts - 1), (cut - 2) & (cuts - 1), cut ^ 1
    far = cut ^ 4
    width = integrals.shape[2]
    span = HUBS * LANES

    tile_copy = pltpu.make_async_copy(amplitudes, tiles, tile_sem)
    tile_copy.start()

    barrier = pltpu.get_barrier_semaphore()

    def greet(offset, carry):
        pl.semaphore_signal(barrier, inc=1, device_id={"blk": moved(group, offset), "cuts": cut}, device_id_type=MESH)
        return carry

    lax.fori_loop(1, groups, greet, 0)
    for other in (high, low, twin):
        pl.semaphore_signal(barrier, inc=1, device_id={"blk": group, "cuts": other}, device_id_type=MESH)
    pl.semaphore_wait(barrier, groups - 1 + 3)
    tile_copy.wait()

    def wait_for(ref, semaphore):
        pltpu.make_async_copy(ref, ref, semaphore).wait()

    def block_copy(j):
        quarter, first, count = chunks[j]
        return pltpu.make_async_copy(
            integrals.at[pl.ds(first, count), pl.ds(quarter * span, span), :], blocks[j], block_sem.at[j]
        )

    def is_hub(quarter):
        return (((group >> 2) + group) & 1) == ((cut + quarter) & 1)

    def spread(quarter):
        half = quarter // 2
        place = middle[half].at[pl.ds(pl.multiple_of(group * 8, 8), 8)]

        def source(index):
            return tiles.at[:, :, pl.ds(pl.multiple_of(quarter * span + index * LANES, LANES), LANES)]

        def remote(step):
            index = ((group >> 1) + step) & (HUBS - 1)
            hub = (index << 1) | (((index >> 1) + cut + quarter) & 1)
            return pltpu.make_async_remote_copy(
                src_ref=source(index),
                dst_ref=place,
                send_sem=spread_send.at[half],
                recv_sem=spread_recv.at[half],
                device_id={"blk": hub, "cuts": cut},
                device_id_type=MESH,
            )

        def one(step, carry):
            remote(step).start()
            return carry

        lax.fori_loop(1, HUBS, one, 0)

        @pl.when(is_hub(quarter))
        def _():
            pltpu.make_async_copy(source(group >> 1), place, spread_recv.at[half]).start()

        @pl.when(jnp.logical_not(is_hub(quarter)))
        def _():
            remote(0).start()

    def sort(j):
        quarter, first, count = chunks[j]
        half = quarter // 2

        @pl.when(is_hub(quarter))
        def _():
            if first == 0:
                wait_for(middle[half], spread_recv.at[half])
            column = pl.multiple_of((group >> 1) * LANES, LANES)
            place = rows[j].at[pl.ds(0, count), pl.ds(pl.multiple_of(cut * 16, 16), 16), pl.ds(column, LANES)]

            def pick(offset):
                target = moved(group, offset)
                live = live_blocks[target]
                for block in range(first, first + count):
                    tile = middle[half][tile_index[target * 8 + block]]
                    leave[half][offset, block] = jnp.where(live > block, tile, jnp.zeros_like(tile))
                return target

            def one(step, carry):
                offset = (step * STRIDE) & 15
                target = pick(offset)
                pltpu.make_async_remote_copy(
                    src_ref=leave[half].at[offset, pl.ds(first, count)],
                    dst_ref=place,
                    send_sem=sort_send.at[half],
                    recv_sem=sort_recv.at[j],
                    device_id={"blk": target, "cuts": cut},
                    device_id_type=MESH,
                ).start()
                return carry

            lax.fori_loop(1, groups, one, 0)
            pick(0)
            pltpu.make_async_copy(leave[half].at[0, pl.ds(first, count)], place, sort_recv.at[j]).start()

        if first == 0 and quarter + 1 < QUARTERS:
            spread(quarter + 1)

    def along(j, owner, target, arrival, side=None):
        columns = pl.ds(0, span) if side is None else pl.ds(side * (span // 2), span // 2)
        view = rows[j].at[:, pl.ds(pl.multiple_of(owner * 16, 16), 16), columns]
        return pltpu.make_async_remote_copy(
            src_ref=view,
            dst_ref=view,
            send_sem=way_sem.at[j],
            recv_sem=arrival.at[j],
            device_id={"blk": group, "cuts": target},
            device_id_type=MESH,
        )

    def piece(j, side=False):
        return rows[j].at[:, pl.ds(0, 16), pl.ds(0, span // (2 if side else 1))]

    def turn(j):
        wait_for(piece(j), sort_recv.at[j])
        along(j, cut, high, from_low).start()
        along(j, cut, low, from_high).start()
        along(j, cut, twin, from_twin).start()
        block_copy(j).start()

    def relay(j):
        wait_for(piece(j), from_low.at[j])
        along(j, low, high, from_low2, 0).start()
        along(j, low, twin, from_twin).start()
        wait_for(piece(j), from_high.at[j])
        along(j, high, low, from_high2, 1).start()
        along(j, high, twin, from_twin).start()

    def finish(j):
        wait_for(piece(j, True), from_low2.at[j])
        along(j, far, twin, from_twin, 0).start()
        wait_for(piece(j, True), from_high2.at[j])
        along(j, far, twin, from_twin, 1).start()

    def multiply(j):
        wait_for(rows[j].at[:, pl.ds(0, 64)], from_twin.at[j])
        block_copy(j).wait()
        product = jnp.dot(rows[j][0], blocks[j][0], preferred_element_type=jnp.float32)
        for block in range(1, chunks[j][2]):
            product += jnp.dot(rows[j][block], blocks[j][block], preferred_element_type=jnp.float32)
        product = product.reshape(total.shape)
        if j == 0:
            total[...] = product
        else:
            total[...] += product

    spread(0)
    for j in range(SORT_AHEAD):
        sort(j)
    for t in range(parts + 3):
        if t + SORT_AHEAD < parts:
            sort(t + SORT_AHEAD)
        if t < parts:
            turn(t)
        if 0 <= t - 1 < parts:
            relay(t - 1)
        if 0 <= t - 2 < parts:
            finish(t - 2)
        if 0 <= t - 3 < parts:
            multiply(t - 3)

    def scatter(offset, carry):
        target = moved(group, offset)
        pltpu.make_async_remote_copy(
            src_ref=total.at[target],
            dst_ref=sums.at[offset],
            send_sem=sum_send,
            recv_sem=sum_recv,
            device_id={"blk": target, "cuts": cut},
            device_id_type=MESH,
        ).start()
        return carry

    lax.fori_loop(1, groups, scatter, 0)
    line = lax.broadcasted_iota(jnp.int32, (8, width), 0)
    energy = jnp.zeros((8, width), jnp.float32)
    for i in range(8):
        pair = group * 8 + i
        energy = jnp.where(line == i, occ[pairs[0, pair]] + occ[pairs[1, pair]], energy)
    denominator = energy - ab[...].reshape(1, width)
    wait_for(sums.at[pl.ds(1, groups - 1)], sum_recv)
    ladder = total[group]
    for offset in range(1, groups):
        ladder = ladder + sums[offset]
    mine[...] = ladder / denominator

    def share(offset, carry):
        pltpu.make_async_remote_copy(
            src_ref=mine,
            dst_ref=out.at[group],
            send_sem=out_send,
            recv_sem=out_recv,
            device_id={"blk": moved(group, offset), "cuts": cut},
            device_id_type=MESH,
        ).start()
        return carry

    lax.fori_loop(1, groups, share, 0)
    keep = pltpu.make_async_copy(mine, out.at[group], end_sem)
    keep.start()
    for half in range(2):
        wait_for(middle[half].at[pl.ds(8, 120)], spread_send.at[half])
        wait_for(leave[half].at[pl.ds(1, groups - 1)], sort_send.at[half])
    for j in range(parts):
        wait_for(rows[j].at[:, pl.ds(0, 112)], way_sem.at[j])
    wait_for(sums.at[pl.ds(1, groups - 1)], sum_send)
    wait_for(sums.at[pl.ds(1, groups - 1)], out_recv)
    wait_for(sums.at[pl.ds(1, groups - 1)], out_send)
    keep.wait()


def on_device(integrals, amplitudes, tile_index, live_blocks, pair_index, occ_energy, ab_energy):
    groups = lax.axis_size("blk")
    per_group, depth, width = integrals.shape
    rows = amplitudes.shape[1]
    pairs = rows * lax.axis_size("cuts")
    part_rows = pairs // groups
    span = HUBS * LANES
    parts = len(CHUNKS)
    smem, vmem, hbm = (pl.BlockSpec(memory_space=space) for space in (pltpu.SMEM, pltpu.VMEM, pl.ANY))
    dma = pltpu.SemaphoreType.DMA
    scratch = [pltpu.VMEM(amplitudes.shape, jnp.bfloat16)]
    scratch += [pltpu.VMEM((groups, part_rows, width), jnp.float32)] * 2
    scratch += [pltpu.VMEM((part_rows, width), jnp.float32)]
    scratch += [pltpu.VMEM((groups * per_group, rows, LANES), jnp.bfloat16)] * 2
    scratch += [pltpu.VMEM((groups, per_group, rows, LANES), jnp.bfloat16)] * 2
    scratch += [pltpu.VMEM((count, span, width), jnp.bfloat16) for _, _, count in CHUNKS]
    scratch += [pltpu.VMEM((count, pairs, span), jnp.bfloat16) for _, _, count in CHUNKS]
    scratch += [dma, dma((parts,)), dma((2,)), dma((2,)), dma((2,)), dma((parts,))] + [dma((parts,))] * 6 + [dma] * 5
    update = pl.pallas_call(
        functools.partial(kernel, CHUNKS),
        out_shape=pltpu.VMEM((groups, part_rows, width), jnp.float32),
        in_specs=[smem, smem, smem, smem, vmem, hbm, hbm],
        out_specs=vmem,
        scratch_shapes=scratch,
        compiler_params=pltpu.CompilerParams(collective_id=0, has_side_effects=True, vmem_limit_bytes=56 << 20),
        cost_estimate=pl.CostEstimate(flops=2 * pairs * per_group * depth * width, bytes_accessed=integrals.size * 2, transcendentals=0),
        name="ladder",
    )(tile_index, live_blocks, pair_index.T, occ_energy, ab_energy, integrals, amplitudes)
    return update.reshape(pairs, width)


def solution(mesh):
    in_specs = (P("blk", None, "cuts"), P("blk", "cuts", None), P(), P(), P(), P(), P("cuts"))
    out_specs = P(None, "cuts")
    return jax.shard_map(
        on_device, mesh=mesh, in_specs=in_specs, out_specs=out_specs, check_vma=False
    )
```

```python
import functools

import jax
import jax.numpy as jnp
from jax import lax
from jax.experimental import pallas as pl
from jax.experimental.pallas import tpu as pltpu
from jax.sharding import PartitionSpec as P

LANES = 128
QUARTERS = 4
HUBS = 8
CHUNKS = tuple((quarter, first, 4) for quarter in range(QUARTERS) for first in range(0, 8, 4))
BANDS = ((0, 256), (256, 128))
TAIL = (2, 2)
PIECES = tuple((j, 0, chunk[2]) for j, chunk in enumerate(CHUNKS[:-1])) + tuple(
    (len(CHUNKS) - 1, sum(TAIL[:i]), size) for i, size in enumerate(TAIL)
)
STRIDE = 5
MESH = pl.DeviceIdType.MESH


def moved(group, offset):
    return ((group + (offset & 12)) & 12) | ((group + offset) & 3)


def kernel(chunks, *refs):
    parts = len(chunks)
    (tile_index, live_blocks, pairs, occ, ab, integrals, amplitudes, out) = refs[:8]
    (tiles, total, sums, mine) = refs[8:12]
    middle, leave = refs[12:14], refs[14:16]
    blocks, rows = refs[16:16 + parts], refs[16 + parts:16 + 2 * parts]
    (tile_sem, block_sem, spread_send, spread_recv, sort_send, sort_recv, way_sem, from_low, from_high, from_low2,
     from_high2, from_twin, sum_send, sum_recv, out_send, out_recv, end_sem) = refs[16 + 2 * parts:]
    groups, cuts = lax.axis_size("blk"), lax.axis_size("cuts")
    group, cut = lax.axis_index("blk"), lax.axis_index("cuts")
    high, low, twin = (cut + 2) & (cuts - 1), (cut - 2) & (cuts - 1), cut ^ 1
    far = cut ^ 4
    width = integrals.shape[2]
    span = HUBS * LANES

    tile_copy = pltpu.make_async_copy(amplitudes, tiles, tile_sem)
    tile_copy.start()

    barrier = pltpu.get_barrier_semaphore()

    def greet(offset, carry):
        pl.semaphore_signal(barrier, inc=1, device_id={"blk": moved(group, offset), "cuts": cut}, device_id_type=MESH)
        return carry

    lax.fori_loop(1, groups, greet, 0)
    for other in (high, low, twin):
        pl.semaphore_signal(barrier, inc=1, device_id={"blk": group, "cuts": other}, device_id_type=MESH)
    pl.semaphore_wait(barrier, groups - 1 + 3)
    tile_copy.wait()

    def wait_for(ref, semaphore):
        pltpu.make_async_copy(ref, ref, semaphore).wait()

    def block_copy(j):
        quarter, first, count = chunks[j]
        return pltpu.make_async_copy(
            integrals.at[pl.ds(first, count), pl.ds(quarter * span, span), :], blocks[j], block_sem.at[j]
        )

    def is_hub(quarter):
        return (((group >> 2) + group) & 1) == ((cut + quarter) & 1)

    def spread(quarter):
        half = quarter // 2
        place = middle[half].at[pl.ds(pl.multiple_of(group * 8, 8), 8)]

        def source(index):
            return tiles.at[:, :, pl.ds(pl.multiple_of(quarter * span + index * LANES, LANES), LANES)]

        def remote(step):
            index = ((group >> 1) + step) & (HUBS - 1)
            hub = (index << 1) | (((index >> 1) + cut + quarter) & 1)
            return pltpu.make_async_remote_copy(
                src_ref=source(index),
                dst_ref=place,
                send_sem=spread_send.at[half],
                recv_sem=spread_recv.at[half],
                device_id={"blk": hub, "cuts": cut},
                device_id_type=MESH,
            )

        def one(step, carry):
            remote(step).start()
            return carry

        lax.fori_loop(1, HUBS, one, 0)

        @pl.when(is_hub(quarter))
        def _():
            pltpu.make_async_copy(source(group >> 1), place, spread_recv.at[half]).start()

        @pl.when(jnp.logical_not(is_hub(quarter)))
        def _():
            remote(0).start()

    def sort(j):
        quarter, first, count = chunks[j]
        half = quarter // 2

        @pl.when(is_hub(quarter))
        def _():
            if first == 0:
                wait_for(middle[half], spread_recv.at[half])
            column = pl.multiple_of((group >> 1) * LANES, LANES)
            place = rows[j].at[pl.ds(0, count), pl.ds(pl.multiple_of(cut * 16, 16), 16), pl.ds(column, LANES)]

            def pick(offset):
                target = moved(group, offset)
                live = live_blocks[target]
                for block in range(first, first + count):
                    tile = middle[half][tile_index[target * 8 + block]]
                    leave[half][offset, block] = jnp.where(live > block, tile, jnp.zeros_like(tile))
                return target

            def one(step, carry):
                offset = (step * STRIDE) & 15
                target = pick(offset)
                pltpu.make_async_remote_copy(
                    src_ref=leave[half].at[offset, pl.ds(first, count)],
                    dst_ref=place,
                    send_sem=sort_send.at[half],
                    recv_sem=sort_recv.at[j],
                    device_id={"blk": target, "cuts": cut},
                    device_id_type=MESH,
                ).start()
                return carry

            lax.fori_loop(1, groups, one, 0)
            pick(0)
            pltpu.make_async_copy(leave[half].at[0, pl.ds(first, count)], place, sort_recv.at[j]).start()

        if first == 0 and quarter + 1 < QUARTERS:
            spread(quarter + 1)

    def along(u, owner, target, arrival, side=None):
        j, first, count = PIECES[u]
        columns = pl.ds(0, span) if side is None else pl.ds(side * (span // 2), span // 2)
        view = rows[j].at[pl.ds(first, count), pl.ds(pl.multiple_of(owner * 16, 16), 16), columns]
        return pltpu.make_async_remote_copy(
            src_ref=view,
            dst_ref=view,
            send_sem=way_sem.at[u],
            recv_sem=arrival.at[u],
            device_id={"blk": group, "cuts": target},
            device_id_type=MESH,
        )

    def piece(u, lines=16, columns=span):
        j, first, count = PIECES[u]
        return rows[j].at[pl.ds(first, count), pl.ds(0, lines), pl.ds(0, columns)]

    def turn(u):
        j, first, _ = PIECES[u]
        if first == 0:
            wait_for(rows[j].at[:, pl.ds(0, 16)], sort_recv.at[j])
        along(u, cut, high, from_low).start()
        along(u, cut, low, from_high).start()
        along(u, cut, twin, from_twin).start()
        if first == 0:
            block_copy(j).start()

    def relay(u):
        wait_for(piece(u), from_low.at[u])
        along(u, low, high, from_low2, 0).start()
        along(u, low, twin, from_twin).start()
        wait_for(piece(u), from_high.at[u])
        along(u, high, low, from_high2, 1).start()
        along(u, high, twin, from_twin).start()

    def finish(u):
        wait_for(piece(u, 16, span // 2), from_low2.at[u])
        along(u, far, twin, from_twin, 0).start()
        wait_for(piece(u, 16, span // 2), from_high2.at[u])
        along(u, far, twin, from_twin, 1).start()

    def multiply(u):
        j, first, count = PIECES[u]
        wait_for(piece(u, 64), from_twin.at[u])
        if first == 0:
            block_copy(j).wait()
        for band in range(len(BANDS)) if u == len(PIECES) - 1 else (None,):
            columns = slice(None) if band is None else pl.ds(*BANDS[band])
            product = jnp.dot(rows[j][first], blocks[j][first, :, columns], preferred_element_type=jnp.float32)
            for block in range(first + 1, first + count):
                product += jnp.dot(rows[j][block], blocks[j][block, :, columns], preferred_element_type=jnp.float32)
            product = product.reshape(groups, 8, product.shape[1])
            if u == 0:
                total[:, :, columns] = product
            else:
                total[:, :, columns] += product
            if band is not None:
                scatter(band)

    def scatter(band):
        columns = pl.ds(*BANDS[band])

        def one(step, carry):
            offset = (step * STRIDE) & 15
            target = moved(group, offset)
            pltpu.make_async_remote_copy(
                src_ref=total.at[target, :, columns],
                dst_ref=sums.at[offset, :, columns],
                send_sem=sum_send.at[band],
                recv_sem=sum_recv.at[band],
                device_id={"blk": target, "cuts": cut},
                device_id_type=MESH,
            ).start()
            return carry

        lax.fori_loop(1, groups, one, 0)

    spread(0)
    sort(0)
    for t in range(parts):
        if t + 1 < parts:
            sort(t + 1)
            turn(t)
        else:
            for u in range(t, len(PIECES)):
                turn(u)
        if t >= 1:
            relay(t - 1)
        if t >= 3:
            multiply(t - 3)
        if t >= 2:
            finish(t - 2)
    last = range(parts - 1, len(PIECES))
    for u in last:
        relay(u)
    multiply(parts - 3)
    finish(parts - 2)
    for u in last:
        finish(u)
    for u in range(parts - 2, len(PIECES)):
        multiply(u)

    line = lax.broadcasted_iota(jnp.int32, (8, width), 0)
    energy = jnp.zeros((8, width), jnp.float32)
    for i in range(8):
        pair = group * 8 + i
        energy = jnp.where(line == i, occ[pairs[0, pair]] + occ[pairs[1, pair]], energy)
    denominator = energy - ab[...].reshape(1, width)

    def others(band):
        return sums.at[pl.ds(1, groups - 1), :, pl.ds(*BANDS[band])]

    def share(band):
        columns = pl.ds(*BANDS[band])
        wait_for(others(band), sum_recv.at[band])
        ladder = total[group, :, columns]
        for offset in range(1, groups):
            ladder = ladder + sums[offset, :, columns]
        mine[:, columns] = ladder / denominator[:, BANDS[band][0]:sum(BANDS[band])]

        def one(step, carry):
            pltpu.make_async_remote_copy(
                src_ref=mine.at[:, columns],
                dst_ref=out.at[group, :, columns],
                send_sem=out_send.at[band],
                recv_sem=out_recv.at[band],
                device_id={"blk": moved(group, (step * STRIDE) & 15), "cuts": cut},
                device_id_type=MESH,
            ).start()
            return carry

        lax.fori_loop(1, groups, one, 0)

    for band in range(len(BANDS)):
        share(band)
    keep = pltpu.make_async_copy(mine, out.at[group], end_sem)
    keep.start()
    for half in range(2):
        wait_for(middle[half].at[pl.ds(8, 120)], spread_send.at[half])
        wait_for(leave[half].at[pl.ds(1, groups - 1)], sort_send.at[half])
    for u in range(len(PIECES)):
        wait_for(piece(u, 112), way_sem.at[u])
    for band in range(len(BANDS)):
        wait_for(others(band), sum_send.at[band])
        wait_for(others(band), out_recv.at[band])
        wait_for(others(band), out_send.at[band])
    keep.wait()


def on_device(integrals, amplitudes, tile_index, live_blocks, pair_index, occ_energy, ab_energy):
    groups = lax.axis_size("blk")
    per_group, depth, width = integrals.shape
    rows = amplitudes.shape[1]
    pairs = rows * lax.axis_size("cuts")
    part_rows = pairs // groups
    span = HUBS * LANES
    parts = len(CHUNKS)
    smem, vmem, hbm = (pl.BlockSpec(memory_space=space) for space in (pltpu.SMEM, pltpu.VMEM, pl.ANY))
    dma = pltpu.SemaphoreType.DMA
    scratch = [pltpu.VMEM(amplitudes.shape, jnp.bfloat16)]
    scratch += [pltpu.VMEM((groups, part_rows, width), jnp.float32)] * 2
    scratch += [pltpu.VMEM((part_rows, width), jnp.float32)]
    scratch += [pltpu.VMEM((groups * per_group, rows, LANES), jnp.bfloat16)] * 2
    scratch += [pltpu.VMEM((groups, per_group, rows, LANES), jnp.bfloat16)] * 2
    scratch += [pltpu.VMEM((count, span, width), jnp.bfloat16) for _, _, count in CHUNKS]
    scratch += [pltpu.VMEM((count, pairs, span), jnp.bfloat16) for _, _, count in CHUNKS]
    scratch += [dma, dma((parts,)), dma((2,)), dma((2,)), dma((2,)), dma((parts,))] + [dma((len(PIECES),))] * 6 + [dma((len(BANDS),))] * 4 + [dma]
    update = pl.pallas_call(
        functools.partial(kernel, CHUNKS),
        out_shape=pltpu.VMEM((groups, part_rows, width), jnp.float32),
        in_specs=[smem, smem, smem, smem, vmem, hbm, hbm],
        out_specs=vmem,
        scratch_shapes=scratch,
        compiler_params=pltpu.CompilerParams(collective_id=0, has_side_effects=True, vmem_limit_bytes=56 << 20),
        cost_estimate=pl.CostEstimate(flops=2 * pairs * per_group * depth * width, bytes_accessed=integrals.size * 2, transcendentals=0),
        name="ladder",
    )(tile_index, live_blocks, pair_index.T, occ_energy, ab_energy, integrals, amplitudes)
    return update.reshape(pairs, width)


def solution(mesh):
    in_specs = (P("blk", None, "cuts"), P("blk", "cuts", None), P(), P(), P(), P(), P("cuts"))
    out_specs = P(None, "cuts")
    return jax.shard_map(
        on_device, mesh=mesh, in_specs=in_specs, out_specs=out_specs, check_vma=False
    )
```

```python
import functools

import jax
import jax.numpy as jnp
from jax import lax
from jax.experimental import pallas as pl
from jax.experimental.pallas import tpu as pltpu
from jax.sharding import PartitionSpec as P

LANES = 128
QUARTERS = 4
HUBS = 8
CHUNKS = tuple((quarter, first, 4) for quarter in range(QUARTERS) for first in range(0, 8, 4))
BANDS = ((0, 256), (256, 128))
TAIL = (2, 2)
PIECES = tuple((j, 0, chunk[2]) for j, chunk in enumerate(CHUNKS[:-1])) + tuple(
    (len(CHUNKS) - 1, sum(TAIL[:i]), size) for i, size in enumerate(TAIL)
)
FAR_FIRST = (10, 6, 9, 11, 14, 2, 8, 5, 7, 13, 15, 1, 3, 4, 12)
MESH = pl.DeviceIdType.MESH


def moved(group, offset):
    return ((group + (offset & 12)) & 12) | ((group + offset) & 3)


def kernel(chunks, *refs):
    parts = len(chunks)
    (tile_index, live_blocks, pairs, occ, ab, integrals, amplitudes, out) = refs[:8]
    (tiles, total, sums, mine) = refs[8:12]
    middle, leave = refs[12:14], refs[14:16]
    blocks, rows = refs[16:16 + parts], refs[16 + parts:16 + 2 * parts]
    (tile_sem, block_sem, spread_send, spread_recv, sort_send, sort_recv, way_sem, from_low, from_high, from_low2,
     from_high2, from_twin, sum_send, sum_recv, out_send, out_recv, end_sem) = refs[16 + 2 * parts:]
    groups, cuts = lax.axis_size("blk"), lax.axis_size("cuts")
    group, cut = lax.axis_index("blk"), lax.axis_index("cuts")
    high, low, twin = (cut + 2) & (cuts - 1), (cut - 2) & (cuts - 1), cut ^ 1
    far = cut ^ 4
    width = integrals.shape[2]
    span = HUBS * LANES

    tile_copy = pltpu.make_async_copy(amplitudes, tiles, tile_sem)
    tile_copy.start()

    barrier = pltpu.get_barrier_semaphore()

    def greet(offset, carry):
        pl.semaphore_signal(barrier, inc=1, device_id={"blk": moved(group, offset), "cuts": cut}, device_id_type=MESH)
        return carry

    lax.fori_loop(1, groups, greet, 0)
    for other in (high, low, twin):
        pl.semaphore_signal(barrier, inc=1, device_id={"blk": group, "cuts": other}, device_id_type=MESH)
    pl.semaphore_wait(barrier, groups - 1 + 3)
    tile_copy.wait()

    def wait_for(ref, semaphore):
        pltpu.make_async_copy(ref, ref, semaphore).wait()

    def block_copy(j):
        quarter, first, count = chunks[j]
        return pltpu.make_async_copy(
            integrals.at[pl.ds(first, count), pl.ds(quarter * span, span), :], blocks[j], block_sem.at[j]
        )

    def is_hub(quarter):
        return (((group >> 2) + group) & 1) == ((cut + quarter) & 1)

    def spread(quarter):
        half = quarter // 2
        place = middle[half].at[pl.ds(pl.multiple_of(group * 8, 8), 8)]

        def source(index):
            return tiles.at[:, :, pl.ds(pl.multiple_of(quarter * span + index * LANES, LANES), LANES)]

        def remote(step):
            index = ((group >> 1) + step) & (HUBS - 1)
            hub = (index << 1) | (((index >> 1) + cut + quarter) & 1)
            return pltpu.make_async_remote_copy(
                src_ref=source(index),
                dst_ref=place,
                send_sem=spread_send.at[half],
                recv_sem=spread_recv.at[half],
                device_id={"blk": hub, "cuts": cut},
                device_id_type=MESH,
            )

        def one(step, carry):
            remote(step).start()
            return carry

        lax.fori_loop(1, HUBS, one, 0)

        @pl.when(is_hub(quarter))
        def _():
            pltpu.make_async_copy(source(group >> 1), place, spread_recv.at[half]).start()

        @pl.when(jnp.logical_not(is_hub(quarter)))
        def _():
            remote(0).start()

    def sort(j):
        quarter, first, count = chunks[j]
        half = quarter // 2

        @pl.when(is_hub(quarter))
        def _():
            if first == 0:
                wait_for(middle[half], spread_recv.at[half])
            column = pl.multiple_of((group >> 1) * LANES, LANES)
            place = rows[j].at[pl.ds(0, count), pl.ds(pl.multiple_of(cut * 16, 16), 16), pl.ds(column, LANES)]

            def pick(offset):
                target = moved(group, offset)
                live = live_blocks[target]
                for block in range(first, first + count):
                    tile = middle[half][tile_index[target * 8 + block]]
                    leave[half][offset, block] = jnp.where(live > block, tile, jnp.zeros_like(tile))
                return target

            def one(offset):
                target = pick(offset)
                pltpu.make_async_remote_copy(
                    src_ref=leave[half].at[offset, pl.ds(first, count)],
                    dst_ref=place,
                    send_sem=sort_send.at[half],
                    recv_sem=sort_recv.at[j],
                    device_id={"blk": target, "cuts": cut},
                    device_id_type=MESH,
                ).start()

            for offset in FAR_FIRST:
                one(offset)
            pick(0)
            pltpu.make_async_copy(leave[half].at[0, pl.ds(first, count)], place, sort_recv.at[j]).start()

        if first == 0 and quarter + 1 < QUARTERS:
            spread(quarter + 1)

    def along(u, owner, target, arrival, side=None):
        j, first, count = PIECES[u]
        columns = pl.ds(0, span) if side is None else pl.ds(side * (span // 2), span // 2)
        view = rows[j].at[pl.ds(first, count), pl.ds(pl.multiple_of(owner * 16, 16), 16), columns]
        return pltpu.make_async_remote_copy(
            src_ref=view,
            dst_ref=view,
            send_sem=way_sem.at[u],
            recv_sem=arrival.at[u],
            device_id={"blk": group, "cuts": target},
            device_id_type=MESH,
        )

    def piece(u, lines=16, columns=span):
        j, first, count = PIECES[u]
        return rows[j].at[pl.ds(first, count), pl.ds(0, lines), pl.ds(0, columns)]

    def turn(u):
        j, first, _ = PIECES[u]
        if first == 0:
            wait_for(rows[j].at[:, pl.ds(0, 16)], sort_recv.at[j])
        along(u, cut, high, from_low).start()
        along(u, cut, low, from_high).start()
        along(u, cut, twin, from_twin).start()
        if first == 0:
            block_copy(j).start()

    def relay(u):
        wait_for(piece(u), from_low.at[u])
        along(u, low, high, from_low2, 0).start()
        along(u, low, twin, from_twin).start()
        wait_for(piece(u), from_high.at[u])
        along(u, high, low, from_high2, 1).start()
        along(u, high, twin, from_twin).start()

    def finish(u):
        wait_for(piece(u, 16, span // 2), from_low2.at[u])
        along(u, far, twin, from_twin, 0).start()
        wait_for(piece(u, 16, span // 2), from_high2.at[u])
        along(u, far, twin, from_twin, 1).start()

    def multiply(u):
        j, first, count = PIECES[u]
        wait_for(piece(u, 64), from_twin.at[u])
        if first == 0:
            block_copy(j).wait()
        for band in range(len(BANDS)) if u == len(PIECES) - 1 else (None,):
            columns = slice(None) if band is None else pl.ds(*BANDS[band])
            product = jnp.dot(rows[j][first], blocks[j][first, :, columns], preferred_element_type=jnp.float32)
            for block in range(first + 1, first + count):
                product += jnp.dot(rows[j][block], blocks[j][block, :, columns], preferred_element_type=jnp.float32)
            product = product.reshape(groups, 8, product.shape[1])
            if u == 0:
                total[:, :, columns] = product
            else:
                total[:, :, columns] += product
            if band is not None:
                scatter(band)

    def scatter(band):
        columns = pl.ds(*BANDS[band])

        def one(offset):
            target = moved(group, offset)
            pltpu.make_async_remote_copy(
                src_ref=total.at[target, :, columns],
                dst_ref=sums.at[offset, :, columns],
                send_sem=sum_send.at[band],
                recv_sem=sum_recv.at[band],
                device_id={"blk": target, "cuts": cut},
                device_id_type=MESH,
            ).start()

        for offset in FAR_FIRST:
            one(offset)

    spread(0)
    sort(0)
    for t in range(parts):
        if t + 1 < parts:
            sort(t + 1)
            turn(t)
        else:
            for u in range(t, len(PIECES)):
                turn(u)
        if t >= 1:
            relay(t - 1)
        if t >= 3:
            multiply(t - 3)
        if t >= 2:
            finish(t - 2)
    last = range(parts - 1, len(PIECES))
    for u in last:
        relay(u)
    multiply(parts - 3)
    finish(parts - 2)
    for u in last:
        finish(u)
    for u in range(parts - 2, len(PIECES)):
        multiply(u)

    line = lax.broadcasted_iota(jnp.int32, (8, width), 0)
    energy = jnp.zeros((8, width), jnp.float32)
    for i in range(8):
        pair = group * 8 + i
        energy = jnp.where(line == i, occ[pairs[0, pair]] + occ[pairs[1, pair]], energy)
    denominator = energy - ab[...].reshape(1, width)

    def others(band):
        return sums.at[pl.ds(1, groups - 1), :, pl.ds(*BANDS[band])]

    def share(band):
        columns = pl.ds(*BANDS[band])
        wait_for(others(band), sum_recv.at[band])
        ladder = total[group, :, columns]
        for offset in range(1, groups):
            ladder = ladder + sums[offset, :, columns]
        mine[:, columns] = ladder / denominator[:, BANDS[band][0]:sum(BANDS[band])]

        def one(offset):
            pltpu.make_async_remote_copy(
                src_ref=mine.at[:, columns],
                dst_ref=out.at[group, :, columns],
                send_sem=out_send.at[band],
                recv_sem=out_recv.at[band],
                device_id={"blk": moved(group, offset), "cuts": cut},
                device_id_type=MESH,
            ).start()

        for offset in FAR_FIRST:
            one(offset)

    for band in range(len(BANDS)):
        share(band)
    keep = pltpu.make_async_copy(mine, out.at[group], end_sem)
    keep.start()
    for half in range(2):
        wait_for(middle[half].at[pl.ds(8, 120)], spread_send.at[half])
        wait_for(leave[half].at[pl.ds(1, groups - 1)], sort_send.at[half])
    for u in range(len(PIECES)):
        wait_for(piece(u, 112), way_sem.at[u])
    for band in range(len(BANDS)):
        wait_for(others(band), sum_send.at[band])
        wait_for(others(band), out_recv.at[band])
        wait_for(others(band), out_send.at[band])
    keep.wait()


def on_device(integrals, amplitudes, tile_index, live_blocks, pair_index, occ_energy, ab_energy):
    groups = lax.axis_size("blk")
    per_group, depth, width = integrals.shape
    rows = amplitudes.shape[1]
    pairs = rows * lax.axis_size("cuts")
    part_rows = pairs // groups
    span = HUBS * LANES
    parts = len(CHUNKS)
    smem, vmem, hbm = (pl.BlockSpec(memory_space=space) for space in (pltpu.SMEM, pltpu.VMEM, pl.ANY))
    dma = pltpu.SemaphoreType.DMA
    scratch = [pltpu.VMEM(amplitudes.shape, jnp.bfloat16)]
    scratch += [pltpu.VMEM((groups, part_rows, width), jnp.float32)] * 2
    scratch += [pltpu.VMEM((part_rows, width), jnp.float32)]
    scratch += [pltpu.VMEM((groups * per_group, rows, LANES), jnp.bfloat16)] * 2
    scratch += [pltpu.VMEM((groups, per_group, rows, LANES), jnp.bfloat16)] * 2
    scratch += [pltpu.VMEM((count, span, width), jnp.bfloat16) for _, _, count in CHUNKS]
    scratch += [pltpu.VMEM((count, pairs, span), jnp.bfloat16) for _, _, count in CHUNKS]
    scratch += [dma, dma((parts,)), dma((2,)), dma((2,)), dma((2,)), dma((parts,))] + [dma((len(PIECES),))] * 6 + [dma((len(BANDS),))] * 4 + [dma]
    update = pl.pallas_call(
        functools.partial(kernel, CHUNKS),
        out_shape=pltpu.VMEM((groups, part_rows, width), jnp.float32),
        in_specs=[smem, smem, smem, smem, vmem, hbm, hbm],
        out_specs=vmem,
        scratch_shapes=scratch,
        compiler_params=pltpu.CompilerParams(collective_id=0, has_side_effects=True, vmem_limit_bytes=56 << 20),
        cost_estimate=pl.CostEstimate(flops=2 * pairs * per_group * depth * width, bytes_accessed=integrals.size * 2, transcendentals=0),
        name="ladder",
    )(tile_index, live_blocks, pair_index.T, occ_energy, ab_energy, integrals, amplitudes)
    return update.reshape(pairs, width)


def solution(mesh):
    in_specs = (P("blk", None, "cuts"), P("blk", "cuts", None), P(), P(), P(), P(), P("cuts"))
    out_specs = P(None, "cuts")
    return jax.shard_map(
        on_device, mesh=mesh, in_specs=in_specs, out_specs=out_specs, check_vma=False
    )
```

```python
import functools

import jax
import jax.numpy as jnp
from jax import lax
from jax.experimental import pallas as pl
from jax.experimental.pallas import tpu as pltpu
from jax.sharding import PartitionSpec as P

LANES = 128
QUARTERS = 4
HUBS = 8
CHUNKS = tuple((quarter, first, 4) for quarter in range(QUARTERS) for first in range(0, 8, 4))
BANDS = ((0, 256), (256, 128))
TAIL = (2, 2)
PIECES = tuple((j, 0, chunk[2]) for j, chunk in enumerate(CHUNKS[:-1])) + tuple(
    (len(CHUNKS) - 1, sum(TAIL[:i]), size) for i, size in enumerate(TAIL)
)
FAR_FIRST = (10, 6, 9, 11, 14, 2, 8, 5, 7, 13, 15, 1, 3, 4, 12)
MESH = pl.DeviceIdType.MESH


def moved(group, offset):
    return ((group + (offset & 12)) & 12) | ((group + offset) & 3)


def kernel(chunks, *refs):
    parts = len(chunks)
    (tile_index, live_blocks, pairs, occ, ab, integrals, amplitudes, out) = refs[:8]
    (tiles, total, sums, mine) = refs[8:12]
    middle, leave = refs[12:14], refs[14:16]
    blocks, rows = refs[16:16 + parts], refs[16 + parts:16 + 2 * parts]
    (tile_sem, block_sem, spread_send, spread_recv, sort_send, sort_recv, way_sem, from_low, from_high, from_low2,
     from_high2, from_twin, sum_send, sum_recv, out_send, out_recv, end_sem) = refs[16 + 2 * parts:]
    groups, cuts = lax.axis_size("blk"), lax.axis_size("cuts")
    group, cut = lax.axis_index("blk"), lax.axis_index("cuts")
    high, low, twin = (cut + 2) & (cuts - 1), (cut - 2) & (cuts - 1), cut ^ 1
    far = cut ^ 4
    width = integrals.shape[2]
    span = HUBS * LANES

    tile_copy = pltpu.make_async_copy(amplitudes, tiles, tile_sem)
    tile_copy.start()

    barrier = pltpu.get_barrier_semaphore()

    def greet(offset):
        pl.semaphore_signal(barrier, inc=1, device_id={"blk": moved(group, offset), "cuts": cut}, device_id_type=MESH)

    for offset in FAR_FIRST:
        greet(offset)
    for other in (high, low, twin):
        pl.semaphore_signal(barrier, inc=1, device_id={"blk": group, "cuts": other}, device_id_type=MESH)
    pl.semaphore_wait(barrier, groups - 1 + 3)
    tile_copy.wait()

    def wait_for(ref, semaphore):
        pltpu.make_async_copy(ref, ref, semaphore).wait()

    def block_copy(j):
        quarter, first, count = chunks[j]
        return pltpu.make_async_copy(
            integrals.at[pl.ds(first, count), pl.ds(quarter * span, span), :], blocks[j], block_sem.at[j]
        )

    def is_hub(quarter):
        return (((group >> 2) + group) & 1) == ((cut + quarter) & 1)

    def spread(quarter):
        half = quarter // 2
        place = middle[half].at[pl.ds(pl.multiple_of(group * 8, 8), 8)]

        def source(index):
            return tiles.at[:, :, pl.ds(pl.multiple_of(quarter * span + index * LANES, LANES), LANES)]

        def remote(step):
            index = ((group >> 1) + step) & (HUBS - 1)
            hub = (index << 1) | (((index >> 1) + cut + quarter) & 1)
            return pltpu.make_async_remote_copy(
                src_ref=source(index),
                dst_ref=place,
                send_sem=spread_send.at[half],
                recv_sem=spread_recv.at[half],
                device_id={"blk": hub, "cuts": cut},
                device_id_type=MESH,
            )

        def one(step, carry):
            remote(step).start()
            return carry

        lax.fori_loop(1, HUBS, one, 0)

        @pl.when(is_hub(quarter))
        def _():
            pltpu.make_async_copy(source(group >> 1), place, spread_recv.at[half]).start()

        @pl.when(jnp.logical_not(is_hub(quarter)))
        def _():
            remote(0).start()

    def sort(j):
        quarter, first, count = chunks[j]
        half = quarter // 2

        @pl.when(is_hub(quarter))
        def _():
            if first == 0:
                wait_for(middle[half], spread_recv.at[half])
            column = pl.multiple_of((group >> 1) * LANES, LANES)
            place = rows[j].at[pl.ds(0, count), pl.ds(pl.multiple_of(cut * 16, 16), 16), pl.ds(column, LANES)]

            def pick(offset):
                target = moved(group, offset)
                live = live_blocks[target]
                for block in range(first, first + count):
                    tile = middle[half][tile_index[target * 8 + block]]
                    leave[half][offset, block] = jnp.where(live > block, tile, jnp.zeros_like(tile))
                return target

            def one(offset):
                target = pick(offset)
                pltpu.make_async_remote_copy(
                    src_ref=leave[half].at[offset, pl.ds(first, count)],
                    dst_ref=place,
                    send_sem=sort_send.at[half],
                    recv_sem=sort_recv.at[j],
                    device_id={"blk": target, "cuts": cut},
                    device_id_type=MESH,
                ).start()

            for offset in FAR_FIRST:
                one(offset)
            pick(0)
            pltpu.make_async_copy(leave[half].at[0, pl.ds(first, count)], place, sort_recv.at[j]).start()

        if first == 0 and quarter + 1 < QUARTERS:
            spread(quarter + 1)

    def along(u, owner, target, arrival, side=None):
        j, first, count = PIECES[u]
        columns = pl.ds(0, span) if side is None else pl.ds(side * (span // 2), span // 2)
        view = rows[j].at[pl.ds(first, count), pl.ds(pl.multiple_of(owner * 16, 16), 16), columns]
        return pltpu.make_async_remote_copy(
            src_ref=view,
            dst_ref=view,
            send_sem=way_sem.at[u],
            recv_sem=arrival.at[u],
            device_id={"blk": group, "cuts": target},
            device_id_type=MESH,
        )

    def piece(u, lines=16, columns=span):
        j, first, count = PIECES[u]
        return rows[j].at[pl.ds(first, count), pl.ds(0, lines), pl.ds(0, columns)]

    def turn(u):
        j, first, _ = PIECES[u]
        if first == 0:
            wait_for(rows[j].at[:, pl.ds(0, 16)], sort_recv.at[j])
        along(u, cut, high, from_low).start()
        along(u, cut, low, from_high).start()
        along(u, cut, twin, from_twin).start()
        if first == 0:
            block_copy(j).start()

    def relay(u):
        wait_for(piece(u), from_low.at[u])
        along(u, low, high, from_low2, 0).start()
        along(u, low, twin, from_twin).start()
        wait_for(piece(u), from_high.at[u])
        along(u, high, low, from_high2, 1).start()
        along(u, high, twin, from_twin).start()

    def finish(u):
        wait_for(piece(u, 16, span // 2), from_low2.at[u])
        along(u, far, twin, from_twin, 0).start()
        wait_for(piece(u, 16, span // 2), from_high2.at[u])
        along(u, far, twin, from_twin, 1).start()

    def multiply(u):
        j, first, count = PIECES[u]
        wait_for(piece(u, 64), from_twin.at[u])
        if first == 0:
            block_copy(j).wait()
        for band in range(len(BANDS)) if u == len(PIECES) - 1 else (None,):
            columns = slice(None) if band is None else pl.ds(*BANDS[band])
            product = jnp.dot(rows[j][first], blocks[j][first, :, columns], preferred_element_type=jnp.float32)
            for block in range(first + 1, first + count):
                product += jnp.dot(rows[j][block], blocks[j][block, :, columns], preferred_element_type=jnp.float32)
            product = product.reshape(groups, 8, product.shape[1])
            if u == 0:
                total[:, :, columns] = product
            else:
                total[:, :, columns] += product
            if band is not None:
                scatter(band)

    def scatter(band):
        columns = pl.ds(*BANDS[band])

        def one(offset):
            target = moved(group, offset)
            pltpu.make_async_remote_copy(
                src_ref=total.at[target, :, columns],
                dst_ref=sums.at[offset, :, columns],
                send_sem=sum_send.at[band],
                recv_sem=sum_recv.at[band],
                device_id={"blk": target, "cuts": cut},
                device_id_type=MESH,
            ).start()

        for offset in FAR_FIRST:
            one(offset)

    spread(0)
    sort(0)
    for t in range(parts):
        if t + 1 < parts:
            sort(t + 1)
            turn(t)
        else:
            for u in range(t, len(PIECES)):
                turn(u)
        if t >= 1:
            relay(t - 1)
        if t >= 3:
            multiply(t - 3)
        if t >= 2:
            finish(t - 2)
    last = range(parts - 1, len(PIECES))
    for u in last:
        relay(u)
    multiply(parts - 3)
    finish(parts - 2)
    for u in last:
        finish(u)
    for u in range(parts - 2, len(PIECES)):
        multiply(u)

    line = lax.broadcasted_iota(jnp.int32, (8, width), 0)
    energy = jnp.zeros((8, width), jnp.float32)
    for i in range(8):
        pair = group * 8 + i
        energy = jnp.where(line == i, occ[pairs[0, pair]] + occ[pairs[1, pair]], energy)
    denominator = energy - ab[...].reshape(1, width)

    def others(band):
        return sums.at[pl.ds(1, groups - 1), :, pl.ds(*BANDS[band])]

    def share(band):
        columns = pl.ds(*BANDS[band])
        wait_for(others(band), sum_recv.at[band])
        ladder = total[group, :, columns]
        for offset in range(1, groups):
            ladder = ladder + sums[offset, :, columns]
        mine[:, columns] = ladder / denominator[:, BANDS[band][0]:sum(BANDS[band])]

        def one(offset):
            pltpu.make_async_remote_copy(
                src_ref=mine.at[:, columns],
                dst_ref=out.at[group, :, columns],
                send_sem=out_send.at[band],
                recv_sem=out_recv.at[band],
                device_id={"blk": moved(group, offset), "cuts": cut},
                device_id_type=MESH,
            ).start()

        for offset in FAR_FIRST:
            one(offset)

    for band in range(len(BANDS)):
        share(band)
    keep = pltpu.make_async_copy(mine, out.at[group], end_sem)
    keep.start()
    for half in range(2):
        wait_for(middle[half].at[pl.ds(8, 120)], spread_send.at[half])
        wait_for(leave[half].at[pl.ds(1, groups - 1)], sort_send.at[half])
    for u in range(len(PIECES)):
        wait_for(piece(u, 112), way_sem.at[u])
    for band in range(len(BANDS)):
        wait_for(others(band), sum_send.at[band])
        wait_for(others(band), out_recv.at[band])
        wait_for(others(band), out_send.at[band])
    keep.wait()


def on_device(integrals, amplitudes, tile_index, live_blocks, pair_index, occ_energy, ab_energy):
    groups = lax.axis_size("blk")
    per_group, depth, width = integrals.shape
    rows = amplitudes.shape[1]
    pairs = rows * lax.axis_size("cuts")
    part_rows = pairs // groups
    span = HUBS * LANES
    parts = len(CHUNKS)
    smem, vmem, hbm = (pl.BlockSpec(memory_space=space) for space in (pltpu.SMEM, pltpu.VMEM, pl.ANY))
    dma = pltpu.SemaphoreType.DMA
    scratch = [pltpu.VMEM(amplitudes.shape, jnp.bfloat16)]
    scratch += [pltpu.VMEM((groups, part_rows, width), jnp.float32)] * 2
    scratch += [pltpu.VMEM((part_rows, width), jnp.float32)]
    scratch += [pltpu.VMEM((groups * per_group, rows, LANES), jnp.bfloat16)] * 2
    scratch += [pltpu.VMEM((groups, per_group, rows, LANES), jnp.bfloat16)] * 2
    scratch += [pltpu.VMEM((count, span, width), jnp.bfloat16) for _, _, count in CHUNKS]
    scratch += [pltpu.VMEM((count, pairs, span), jnp.bfloat16) for _, _, count in CHUNKS]
    scratch += [dma, dma((parts,)), dma((2,)), dma((2,)), dma((2,)), dma((parts,))] + [dma((len(PIECES),))] * 6 + [dma((len(BANDS),))] * 4 + [dma]
    update = pl.pallas_call(
        functools.partial(kernel, CHUNKS),
        out_shape=pltpu.VMEM((groups, part_rows, width), jnp.float32),
        in_specs=[smem, smem, smem, smem, vmem, hbm, hbm],
        out_specs=vmem,
        scratch_shapes=scratch,
        compiler_params=pltpu.CompilerParams(collective_id=0, has_side_effects=True, vmem_limit_bytes=56 << 20),
        cost_estimate=pl.CostEstimate(flops=2 * pairs * per_group * depth * width, bytes_accessed=integrals.size * 2, transcendentals=0),
        name="ladder",
    )(tile_index, live_blocks, pair_index.T, occ_energy, ab_energy, integrals, amplitudes)
    return update.reshape(pairs, width)


def solution(mesh):
    in_specs = (P("blk", None, "cuts"), P("blk", "cuts", None), P(), P(), P(), P(), P("cuts"))
    out_specs = P(None, "cuts")
    return jax.shard_map(
        on_device, mesh=mesh, in_specs=in_specs, out_specs=out_specs, check_vma=False
    )
```
